512 devices in a mesh: expert: 64 (over x, y, core), tensor: 8 (over z).
Axes of the slice: x: 4, y: 8, z: 8, core: 2. Of those that a mesh axis runs over, the one named last changes fastest.
Arguments:
- tokens: bfloat16 [8192, 5120], P('expert', 'tensor'), may hold values from -6 to 6
- out_grad: bfloat16 [8192, 5120], P('expert', 'tensor'), may hold values from -6 to 6
- expert_ids: int32 [8192, 2], P('expert'), may hold values from 0 to 15, all different within a row; in each aligned block of 128 rows (0 to 127, 128 to 255, ...) at most 17 rows name the same one
- gate_probs: float32 [8192, 2], P('expert'), may hold values from 0.2 to 1
- w_gate: bfloat16 [5120, 38912], P('tensor', 'expert'), may hold values from -0.078125 to 0.078125
- w_up: bfloat16 [5120, 38912], P('tensor', 'expert'), may hold values from -0.078125 to 0.078125
- w_down: bfloat16 [38912, 5120], P('expert', 'tensor'), may hold values from -0.125 to 0.125
Outputs:
- grad_tokens: bfloat16 [8192, 5120], P('expert', 'tensor')
- grad_gate: bfloat16 [5120, 38912], P('tensor', 'expert')
- grad_up: bfloat16 [5120, 38912], P('tensor', 'expert')
- grad_down: bfloat16 [38912, 5120], P('expert', 'tensor')
The draws below stay inside these ranges and needn't reach their ends.
Inputs may be any that keep to these rules, and one draw needn't show every extreme that they name: `expert_ids`: each row names two different experts. Among the tokens of one index of the expert axis (aligned blocks of 128 rows) no expert is named more than 17 times, and in every draw some expert is named exactly 17 times in some block.
All inputs are finite; a program needn't handle non-finite values.
Results may differ from the reference program's by a relative error of at most 0.029.
Values may be sent and summed in bfloat16 or wider, within the bound.
No kernel may reach another device: no remote copies, remote signals or barrier semaphores. Data moves between devices by JAX's collectives and lax.ppermute only.
A program may use at most 64 MiB of HBM per device.

```python
import math
import jax
import jax.numpy as jnp
import numpy as np
from jax import lax

D = 5120
FE = 2432
MEMBERS = 4
TOK_DEV = 128
EXPERTS = 16
TOKENS = 8192
CAP = 17
N_EXPERT = 64
N_TENSOR = 8


def steps_of(stream_key, extent, shards, least, largest):
    loudness, own = 1.0, jax.random.fold_in(stream_key, 6)
    for dim, shards_of in shards:
        steps = jnp.exp(jax.random.uniform(jax.random.fold_in(own, dim), (shards_of,), jnp.float32, least / len(shards), largest / len(shards)))
        loudness = loudness * jnp.repeat(steps, extent[dim] // shards_of).reshape([-1 if axis == dim else 1 for axis in range(len(extent))])
    return loudness


def assign_block(own_key, own, number, rows, count, top, most, slope):
    order = jax.random.permutation(own_key, count)
    heavy_load, common = shares(count, rows * top, most, slope, True), shares(count, rows * top, most, slope, False)
    places = jnp.arange(count)

    def named(lengths, turn):
        used = int((lengths > 0).sum())
        fixed = max(1, used // 4)
        shifted = fixed + (places - fixed + turn * (used - fixed)) % max(1, count - fixed)
        return jnp.zeros((count,), jnp.int32).at[order[jnp.where(places < fixed, places, shifted)]].set(jnp.asarray(lengths, jnp.int32))

    lengths = jnp.where(number % 4 == 0, named(heavy_load, number // 4), named(common, number - number // 4 - 1))
    mixed = jax.random.permutation(jax.random.fold_in(own, 3), count)
    donor, receiver = mixed[0:count // 2 * 2:2], mixed[1:count // 2 * 2:2]
    slack = jnp.minimum(lengths[donor] - 1, most - lengths[receiver]) // 2
    slack = jnp.where((donor == order[0]) | (receiver == order[0]) | (lengths[receiver] == 0), 0, jnp.maximum(slack, 0))
    shifted = jax.random.randint(jax.random.fold_in(own, 4), (count // 2,), 0, 1 << 20) % (slack + 1)
    lengths = lengths.at[donor].add(-shifted).at[receiver].add(shifted)
    labels = jnp.searchsorted(jnp.cumsum(lengths), jnp.arange(rows * top), side="right").astype(jnp.int32)
    grid = labels.reshape(top, rows).T
    grid = grid[jax.random.permutation(jax.random.fold_in(own, 1), rows)]
    turn = jax.random.randint(jax.random.fold_in(own, 2), (rows, 1), 0, top)
    return jnp.take_along_axis(grid, (jnp.arange(top)[None, :] + turn) % top, axis=1)


def shares(count, total, bound, lean, full):
    weights = [(1 << 20) // math.isqrt(rank ** lean) + 1 for rank in range(1, count + 1)]
    largest = bound if full else min(bound, max(-(-total // count), total * weights[0] // sum(weights)))
    least = 1 if total - largest >= count - 1 else 0
    given, spare = [largest] + [least] * (count - 1), total - largest - least * (count - 1)
    while spare > 0:
        movable = [i for i in range(1, count) if given[i] < largest] or [i for i in range(1, count) if given[i] < bound]
        pool, left = sum([weights[i] for i in movable]), spare
        for i in movable:
            addition = min(bound - given[i], max(1, left * weights[i] // pool), spare)
            given[i] = given[i] + addition
            spare = spare - addition
    return np.array(given)


def centred(key, dims, scale, bound, pieces=(), held_as=jnp.bfloat16):
    values = scale * jax.random.normal(key, dims, jnp.float32)
    if pieces:
        values = values * steps_of(key, dims, pieces, -0.22, 0.18)
    return jnp.clip(values, -bound, bound).astype(held_as)


def setup_inputs(seed: int = 0) -> dict:
    arg_keys = jax.random.split(jax.random.key(seed), 8)
    tokens = centred(arg_keys[0], (TOKENS, D), 1.0, 6.0, ((0, 64), (1, 8)))
    out_grad = centred(arg_keys[1], (TOKENS, D), 1.0, 6.0, ((0, 64), (1, 8)))
    expert_ids_keys = jax.random.split(jax.random.fold_in(arg_keys[2], 1), TOKENS // TOK_DEV)
    expert_ids_turns = jax.random.permutation(jax.random.fold_in(arg_keys[2], 3), TOKENS // TOK_DEV)
    expert_ids = jax.vmap(lambda own, number: assign_block(jax.random.fold_in(arg_keys[2], 2), own, number, TOK_DEV, EXPERTS, 2, CAP, 2))(expert_ids_keys, expert_ids_turns).reshape((TOKENS, 2))
    gate_probs = jnp.clip(0.2 + 0.8 * jax.random.uniform(arg_keys[3], (TOKENS, 2), jnp.float32) ** steps_of(arg_keys[3], (TOKENS, 2), ((0, 64),), -0.2, 0.2), 0.2, 1.0)
    w_gate = centred(arg_keys[4], (D, EXPERTS * FE), D ** -0.5, 0.078125, ((0, 8), (1, 64)))
    w_up = centred(arg_keys[5], (D, EXPERTS * FE), D ** -0.5, 0.078125, ((0, 8), (1, 64)))
    w_down = centred(arg_keys[6], (EXPERTS * FE, D), FE ** -0.5, 0.125, ((0, 64), (1, 8)))
    return dict(tokens=tokens, out_grad=out_grad, expert_ids=expert_ids, gate_probs=gate_probs, w_gate=w_gate, w_up=w_up, w_down=w_down)


def feature_total_sum(left, right):
    rows = left.shape[0]
    width = right.shape[1]
    group = D // N_TENSOR
    left_operand = left.astype(jnp.float32).reshape(rows, N_TENSOR, group)
    right_operand = right.astype(jnp.float32).reshape(N_TENSOR, group, width)
    piece_list = jnp.einsum("kwl,wlb->wkb", left_operand, right_operand)
    rounded = lax.optimization_barrier(piece_list.astype(jnp.bfloat16))
    return jnp.sum(rounded.astype(jnp.float32), axis=0)


def member_rows(grad_act_gate, grad_act_up, gate_w, up_w):
    rows = grad_act_gate.shape[0]
    share = FE // MEMBERS
    left_gate = grad_act_gate.astype(jnp.float32).reshape(rows, MEMBERS, share)
    left_up = grad_act_up.astype(jnp.float32).reshape(rows, MEMBERS, share)
    right_gate = gate_w.T.astype(jnp.float32).reshape(MEMBERS, share, D)
    right_up_matrix = up_w.T.astype(jnp.float32).reshape(MEMBERS, share, D)
    piece_list = jnp.einsum("rmf,mfd->mrd", left_gate, right_gate) + jnp.einsum("rmf,mfd->mrd", left_up, right_up_matrix)
    rounded = lax.optimization_barrier(piece_list.astype(jnp.bfloat16))
    return jnp.sum(rounded.astype(jnp.float32), axis=0)


def reference(tokens, out_grad, expert_ids, gate_probs, w_gate, w_up, w_down):
    assigned = TOKENS * 2
    limit = N_EXPERT * CAP
    flat_ids = expert_ids.reshape(-1)
    flat_probs = gate_probs.reshape(-1)

    def one_expert(total, expert):
        member = flat_ids == expert
        position = jnp.cumsum(member.astype(jnp.int32)) - 1
        where_to = jnp.where(member, position, limit).astype(jnp.int32)
        picked = jnp.zeros((limit,), jnp.int32).at[where_to].set(jnp.arange(assigned, dtype=jnp.int32), mode="drop")
        valid = jnp.arange(limit, dtype=jnp.int32) < jnp.sum(member.astype(jnp.int32))
        rows_of_tokens = picked // 2
        rows_x = jnp.where(valid[:, None], tokens[rows_of_tokens], jnp.zeros((), tokens.dtype))
        probs_rows = jnp.where(valid, flat_probs[picked], jnp.float32(0.0))
        scaled = (out_grad[rows_of_tokens].astype(jnp.float32) * probs_rows[:, None]).astype(jnp.bfloat16)
        start = (expert * FE).astype(jnp.int32)
        gate_w = lax.dynamic_slice_in_dim(w_gate, start, FE, 1)
        up_w = lax.dynamic_slice_in_dim(w_up, start, FE, 1)
        down_w = lax.dynamic_slice_in_dim(w_down, start, FE, 0)
        gate = feature_total_sum(rows_x, gate_w)
        up = feature_total_sum(rows_x, up_w)
        sigma = jax.nn.sigmoid(gate)
        silu = gate * sigma
        hidden = (silu * up).astype(jnp.bfloat16)
        grad_hidden = feature_total_sum(scaled, down_w.T)
        grad_act_gate = (grad_hidden * up * sigma * (1.0 + gate * (1.0 - sigma))).astype(jnp.bfloat16)
        grad_act_up = (grad_hidden * silu).astype(jnp.bfloat16)
        grad_down = jnp.dot(hidden.T, scaled, preferred_element_type=jnp.float32).astype(jnp.bfloat16)
        grad_gate = jnp.dot(rows_x.T, grad_act_gate, preferred_element_type=jnp.float32).astype(jnp.bfloat16)
        grad_up = jnp.dot(rows_x.T, grad_act_up, preferred_element_type=jnp.float32).astype(jnp.bfloat16)
        partial_rows = member_rows(grad_act_gate, grad_act_up, gate_w, up_w)
        partial_rows = jnp.where(valid[:, None], partial_rows, jnp.float32(0.0))
        total = total.at[picked].add(partial_rows)
        return total, (grad_gate, grad_up, grad_down)

    start_total = jnp.zeros((assigned, D), jnp.float32)
    total, stacked = lax.scan(one_expert, start_total, jnp.arange(EXPERTS, dtype=jnp.int32))
    stacked_gate, stacked_up, stacked_down = stacked
    grad_tokens = total.reshape(TOKENS, 2, D).sum(axis=1).astype(jnp.bfloat16)
    grad_gate = jnp.transpose(stacked_gate, (1, 0, 2)).reshape(D, EXPERTS * FE)
    grad_up = jnp.transpose(stacked_up, (1, 0, 2)).reshape(D, EXPERTS * FE)
    grad_down = stacked_down.reshape(EXPERTS * FE, D)
    return (grad_tokens, grad_gate, grad_up, grad_down)
```

```python
import jax
import jax.numpy as jnp
from jax import lax
from jax.sharding import PartitionSpec as P

MEMBERS = 4
CORES = 2
CAP = 17
MAIN = 16
SENT = 40
LANES = 128
BACK = 24


def activations(gate, up, grad_hidden):
    sigma = jax.nn.sigmoid(gate)
    silu = gate * sigma
    hidden = (silu * up).astype(jnp.bfloat16)
    grad_act_gate = (grad_hidden * up * sigma * (1.0 + gate * (1.0 - sigma))).astype(jnp.bfloat16)
    grad_act_up = (grad_hidden * silu).astype(jnp.bfloat16)
    return (hidden, grad_act_gate, grad_act_up)


def matmul(a, b, a_dim=1, b_dim=0):
    return lax.dot_general(
        a, b, (((a_dim,), (b_dim,)), ((), ())), preferred_element_type=jnp.float32
    )


def on_device(tokens, out_grad, expert_ids, gate_probs, w_gate, w_up, w_down):
    bf16 = jnp.bfloat16
    count, columns = tokens.shape
    devices = lax.axis_size("expert")
    chips = devices // CORES
    groups = devices // MEMBERS
    same_core = [[core + CORES * chip for chip in range(chips)] for core in range(CORES)]
    other_core = [(device, device ^ 1) for device in range(devices)]

    ids = expert_ids.T
    experts = jnp.arange(groups, dtype=jnp.int32)[:, None]
    first, second = ids[0][None, :] == experts, ids[1][None, :] == experts
    named = first | second
    before = (
        jnp.arange(count, dtype=jnp.int32)[:, None] < jnp.arange(count, dtype=jnp.int32)[None, :]
    )
    rank = matmul(named.astype(bf16), before.astype(bf16)).astype(jnp.int32)
    place = jnp.where(named, rank, -1)

    row = jnp.arange(SENT, dtype=jnp.int32)
    slot = jnp.where(row < 2 * MAIN, row % MAIN, MAIN)
    is_x = (row < MAIN) | (row == 2 * MAIN)
    is_grad = ((row >= MAIN) & (row < 2 * MAIN)) | (row == 2 * MAIN + 1)

    def chosen(mask, kind):
        hit = (jnp.where(mask, place, -1)[:, None, :] == slot[None, :, None]) & kind[None, :, None]
        hit = jnp.broadcast_to(hit[:, None], (groups, CORES, SENT, count))
        return hit.reshape(chips * SENT, count).astype(bf16)

    placing = jnp.concatenate(
        [chosen(named, is_x), chosen(first, is_grad), chosen(second, is_grad)], axis=1
    )
    wide = out_grad.astype(jnp.float32)
    rows = jnp.concatenate(
        [
            tokens,
            (wide * gate_probs[:, 0:1]).astype(bf16),
            (wide * gate_probs[:, 1:2]).astype(bf16),
        ],
        axis=0,
    )
    send = matmul(placing, rows).astype(bf16).reshape(chips, SENT, columns)
    mine = lax.all_to_all(
        send, "expert", split_axis=0, concat_axis=0, tiled=True, axis_index_groups=same_core
    )
    theirs = lax.ppermute(mine, "expert", other_core)

    half = chips * MAIN
    both = CORES * half

    def gathered(main, last):
        return jnp.concatenate(
            [
                mine[:, main : main + MAIN].reshape(half, columns),
                theirs[:, main : main + MAIN].reshape(half, columns),
                mine[:, last],
                theirs[:, last],
            ],
            axis=0,
        )

    local_x = gathered(0, 2 * MAIN)
    local_grad = gathered(MAIN, 2 * MAIN + 1)

    hidden_units = w_gate.shape[1]
    width = -(-hidden_units // LANES) * LANES
    pad = ((0, 0), (0, width - hidden_units))
    w_both = jnp.concatenate([jnp.pad(w_gate, pad), jnp.pad(w_up, pad)], axis=1)
    parts = jnp.concatenate(
        [
            matmul(local_x, w_both).astype(bf16),
            matmul(local_grad, jnp.pad(w_down, pad[::-1]), 1, 1).astype(bf16),
        ],
        axis=1,
    )
    sums = lax.psum_scatter(parts, "tensor", scatter_dimension=0, tiled=True).astype(jnp.float32)
    gate, up, grad_hidden = (sums[:, k * width : (k + 1) * width] for k in range(3))
    hidden, grad_act_gate, grad_act_up = activations(gate, up, grad_hidden)

    def spread(part):
        return lax.all_gather(part, "tensor", axis=0, tiled=True)

    cut = hidden_units - LANES
    most = spread(hidden[:, :cut])
    acts = spread(
        jnp.concatenate([grad_act_gate, grad_act_up, hidden[:, cut:hidden_units]], axis=1)
    )
    most, acts = lax.optimization_barrier((most, acts))
    acts, least = acts[:, : 2 * width], acts[:, 2 * width :]
    grad_down = jnp.concatenate(
        [matmul(part, local_grad, 0, 0).astype(bf16) for part in (most, least)], axis=0
    )
    grad_gate = matmul(local_x, acts[:, :hidden_units], 0, 0).astype(bf16)
    grad_up = matmul(local_x, acts[:, width : width + hidden_units], 0, 0).astype(bf16)

    partial = matmul(acts, w_both, 1, 1)
    away = jnp.concatenate([partial[half:both], partial[both + chips :]], axis=0).astype(bf16)
    here = jnp.concatenate([partial[:half], partial[both : both + chips]], axis=0)
    chip_rows = (here + lax.ppermute(away, "expert", other_core).astype(jnp.float32)).astype(bf16)
    back = jnp.concatenate(
        [
            chip_rows[:half].reshape(chips, MAIN, columns),
            chip_rows[half:][:, None],
            jnp.zeros((chips, BACK - CAP, columns), bf16),
        ],
        axis=1,
    )
    returned = lax.all_to_all(
        back, "expert", split_axis=0, concat_axis=0, tiled=True, axis_index_groups=same_core
    ).reshape(chips * BACK, columns)
    taking = place[:, None, None, :] == jnp.arange(BACK, dtype=jnp.int32)[None, None, :, None]
    taking = jnp.broadcast_to(taking, (groups, CORES, BACK, count)).reshape(chips * BACK, count)
    grad_tokens = matmul(taking.astype(bf16), returned, 0, 0).astype(bf16)
    return (grad_tokens, grad_gate, grad_up, grad_down)


def solution(mesh):
    placed = (
        P("expert", "tensor"),
        P("expert", "tensor"),
        P("expert", None),
        P("expert", None),
        P("tensor", "expert"),
        P("tensor", "expert"),
        P("expert", "tensor"),
    )
    return jax.shard_map(
        on_device,
        mesh=mesh,
        in_specs=placed,
        out_specs=(
            P("expert", "tensor"),
            P("tensor", "expert"),
            P("tensor", "expert"),
            P("expert", "tensor"),
        ),
        check_vma=False,
    )
```

```python
import jax
import jax.numpy as jnp
from jax import lax
from jax.sharding import PartitionSpec as P

MEMBERS = 4
CORES = 2
MAIN = 16
SUBLANES = 8
LANES = 128


def activations(gate, up, grad_hidden):
    sigma = jax.nn.sigmoid(gate)
    silu = gate * sigma
    hidden = (silu * up).astype(jnp.bfloat16)
    grad_act_gate = (grad_hidden * up * sigma * (1.0 + gate * (1.0 - sigma))).astype(jnp.bfloat16)
    grad_act_up = (grad_hidden * silu).astype(jnp.bfloat16)
    return (hidden, grad_act_gate, grad_act_up)


def matmul(a, b, a_dim=1, b_dim=0):
    return lax.dot_general(
        a, b, (((a_dim,), (b_dim,)), ((), ())), preferred_element_type=jnp.float32
    )


def on_device(tokens, out_grad, expert_ids, gate_probs, w_gate, w_up, w_down):
    bf16 = jnp.bfloat16
    count, columns = tokens.shape
    devices = lax.axis_size("expert")
    chips = devices // CORES
    groups = devices // MEMBERS
    same_core = [[core + CORES * chip for chip in range(chips)] for core in range(CORES)]
    other_core = [(device, device ^ 1) for device in range(devices)]

    ids = expert_ids.T
    experts = jnp.arange(groups, dtype=jnp.int32)[:, None]
    first, second = ids[0][None, :] == experts, ids[1][None, :] == experts
    named = first | second
    before = (
        jnp.arange(count, dtype=jnp.int32)[:, None] < jnp.arange(count, dtype=jnp.int32)[None, :]
    )
    rank = matmul(named.astype(bf16), before.astype(bf16)).astype(jnp.int32)
    place = jnp.where(named, rank, -1)

    main_slot = jnp.arange(MAIN, dtype=jnp.int32)[None, :, None]

    def chosen(mask):
        held = jnp.where(mask, place, -1)
        main = jnp.broadcast_to(
            (held[:, None, :] == main_slot)[:, None], (groups, CORES, MAIN, count)
        ).reshape(chips * MAIN, count)
        last = jnp.broadcast_to((held == MAIN)[:, None], (groups, CORES, count))
        return main.astype(bf16), last.reshape(chips, count).astype(bf16)

    blocks = columns // LANES
    tiles = MAIN // SUBLANES

    def fold(main, last):
        main = main.reshape(chips, tiles, SUBLANES, blocks, LANES).transpose(0, 1, 3, 2, 4)
        main = main.reshape(chips, MAIN * blocks, LANES)
        last = last.reshape(chips, blocks, LANES)
        spare = jnp.zeros((chips, -blocks % SUBLANES, LANES), last.dtype)
        return jnp.concatenate([main, last, spare], axis=1)

    def unfold(rows):
        main = rows[:, : MAIN * blocks].reshape(chips, tiles, blocks, SUBLANES, LANES)
        main = main.transpose(0, 1, 3, 2, 4).reshape(chips * MAIN, columns)
        return main, rows[:, MAIN * blocks : MAIN * blocks + blocks].reshape(chips, columns)

    def exchange(rows):
        return lax.all_to_all(
            rows, "expert", split_axis=0, concat_axis=0, tiled=True, axis_index_groups=same_core
        )

    def routed(send):
        mine = exchange(send)
        theirs = lax.ppermute(mine, "expert", other_core)
        (main_a, last_a), (main_b, last_b) = unfold(mine), unfold(theirs)
        return jnp.concatenate([main_a, main_b, last_a, last_b], axis=0)

    half = chips * MAIN
    both = CORES * half
    send_x = fold(*(matmul(part, tokens).astype(bf16) for part in chosen(named)))
    wide = out_grad.astype(jnp.float32)
    scaled = jnp.concatenate(
        [
            (wide * gate_probs[:, 0:1]).astype(bf16),
            (wide * gate_probs[:, 1:2]).astype(bf16),
        ],
        axis=0,
    )
    send_grad = fold(
        *(
            matmul(jnp.concatenate(pair, axis=1), scaled).astype(bf16)
            for pair in zip(chosen(first), chosen(second), strict=True)
        )
    )
    local_x = routed(send_x)

    hidden_units = w_gate.shape[1]
    width = -(-hidden_units // LANES) * LANES
    pad = ((0, 0), (0, width - hidden_units))
    w_both = jnp.concatenate([jnp.pad(w_gate, pad), jnp.pad(w_up, pad)], axis=1)
    parts = matmul(local_x, w_both).astype(bf16)
    parts, send_grad = lax.optimization_barrier((parts, send_grad))
    sums = lax.psum_scatter(parts, "tensor", scatter_dimension=0, tiled=True).astype(jnp.float32)
    gate, up = sums[:, :width], sums[:, width:]

    local_grad = routed(send_grad)
    shards = lax.axis_size("tensor")
    pieces = matmul(local_grad, jnp.pad(w_down, pad[::-1]), 1, 1).astype(bf16)
    pieces = lax.all_to_all(
        pieces.reshape(shards, pieces.shape[0] // shards, width),
        "tensor",
        split_axis=0,
        concat_axis=0,
        tiled=True,
    )
    grad_hidden = jnp.sum(pieces.astype(jnp.float32), axis=0)
    hidden, grad_act_gate, grad_act_up = activations(gate, up, grad_hidden)

    def spread(part):
        return lax.all_gather(part, "tensor", axis=0, tiled=True)

    cut = hidden_units - LANES
    most = spread(hidden[:, :cut])
    acts = spread(
        jnp.concatenate([grad_act_gate, grad_act_up, hidden[:, cut:hidden_units]], axis=1)
    )
    most, acts = lax.optimization_barrier((most, acts))
    acts, least = acts[:, : 2 * width], acts[:, 2 * width :]
    grad_down = jnp.concatenate(
        [matmul(part, local_grad, 0, 0).astype(bf16) for part in (most, least)], axis=0
    )
    grad_gate = matmul(local_x, acts[:, :hidden_units], 0, 0).astype(bf16)
    grad_up = matmul(local_x, acts[:, width : width + hidden_units], 0, 0).astype(bf16)

    partial = matmul(acts, w_both, 1, 1)
    away = jnp.concatenate([partial[half:both], partial[both + chips :]], axis=0).astype(bf16)
    here = jnp.concatenate([partial[:half], partial[both : both + chips]], axis=0)
    chip_rows = (here + lax.ppermute(away, "expert", other_core).astype(jnp.float32)).astype(bf16)
    returned = jnp.concatenate(unfold(exchange(fold(chip_rows[:half], chip_rows[half:]))), axis=0)
    taking = jnp.concatenate(chosen(named), axis=0)
    grad_tokens = matmul(taking, returned, 0, 0).astype(bf16)
    return (grad_tokens, grad_gate, grad_up, grad_down)


def solution(mesh):
    placed = (
        P("expert", "tensor"),
        P("expert", "tensor"),
        P("expert", None),
        P("expert", None),
        P("tensor", "expert"),
        P("tensor", "expert"),
        P("expert", "tensor"),
    )
    return jax.shard_map(
        on_device,
        mesh=mesh,
        in_specs=placed,
        out_specs=(
            P("expert", "tensor"),
            P("tensor", "expert"),
            P("tensor", "expert"),
            P("expert", "tensor"),
        ),
        check_vma=False,
    )
```

```python
import jax
import jax.numpy as jnp
from jax import lax
from jax.sharding import PartitionSpec as P

MEMBERS = 4
CORES = 2
MAIN = 16
SUBLANES = 8
LANES = 128


def activations(gate, up, grad_hidden):
    sigma = jax.nn.sigmoid(gate)
    silu = gate * sigma
    hidden = (silu * up).astype(jnp.bfloat16)
    grad_act_gate = (grad_hidden * up * sigma * (1.0 + gate * (1.0 - sigma))).astype(jnp.bfloat16)
    grad_act_up = (grad_hidden * silu).astype(jnp.bfloat16)
    return (hidden, grad_act_gate, grad_act_up)


def matmul(a, b, a_dim=1, b_dim=0):
    return lax.dot_general(
        a, b, (((a_dim,), (b_dim,)), ((), ())), preferred_element_type=jnp.float32
    )


def on_device(tokens, out_grad, expert_ids, gate_probs, w_gate, w_up, w_down):
    bf16 = jnp.bfloat16
    count, columns = tokens.shape
    devices = lax.axis_size("expert")
    chips = devices // CORES
    groups = devices // MEMBERS
    same_core = [[core + CORES * chip for chip in range(chips)] for core in range(CORES)]
    other_core = [(device, device ^ 1) for device in range(devices)]

    ids = expert_ids.T
    experts = jnp.arange(groups, dtype=jnp.int32)[:, None]
    first, second = ids[0][None, :] == experts, ids[1][None, :] == experts
    named = first | second
    before = (
        jnp.arange(count, dtype=jnp.int32)[:, None] < jnp.arange(count, dtype=jnp.int32)[None, :]
    )
    rank = matmul(named.astype(bf16), before.astype(bf16)).astype(jnp.int32)
    place = jnp.where(named, rank, -1)

    main_slot = jnp.arange(MAIN, dtype=jnp.int32)[None, :, None]

    def chosen(mask):
        held = jnp.where(mask, place, -1)
        main = jnp.broadcast_to(
            (held[:, None, :] == main_slot)[:, None], (groups, CORES, MAIN, count)
        ).reshape(chips * MAIN, count)
        last = jnp.broadcast_to((held == MAIN)[:, None], (groups, CORES, count))
        return main.astype(bf16), last.reshape(chips, count).astype(bf16)

    blocks = columns // LANES
    tiles = MAIN // SUBLANES

    def fold(main, last):
        main = main.reshape(chips, tiles, SUBLANES, blocks, LANES).transpose(0, 1, 3, 2, 4)
        main = main.reshape(chips, MAIN * blocks, LANES)
        last = last.reshape(chips, blocks, LANES)
        spare = jnp.zeros((chips, -blocks % SUBLANES, LANES), last.dtype)
        return jnp.concatenate([main, last, spare], axis=1)

    def unfold(rows):
        main = rows[:, : MAIN * blocks].reshape(chips, tiles, blocks, SUBLANES, LANES)
        main = main.transpose(0, 1, 3, 2, 4).reshape(chips * MAIN, columns)
        return main, rows[:, MAIN * blocks : MAIN * blocks + blocks].reshape(chips, columns)

    def exchange(rows):
        return lax.all_to_all(
            rows, "expert", split_axis=0, concat_axis=0, tiled=True, axis_index_groups=same_core
        )

    def routed(send):
        mine = exchange(send)
        theirs = lax.ppermute(mine, "expert", other_core)
        (main_a, last_a), (main_b, last_b) = unfold(mine), unfold(theirs)
        return jnp.concatenate([main_a, last_a, main_b, last_b], axis=0)

    main = chips * MAIN
    half = main + chips
    send_x = fold(*(matmul(part, tokens).astype(bf16) for part in chosen(named)))
    send_x, out_grad, gate_probs = lax.optimization_barrier((send_x, out_grad, gate_probs))
    wide = out_grad.astype(jnp.float32)
    scaled = jnp.concatenate(
        [
            (wide * gate_probs[:, 0:1]).astype(bf16),
            (wide * gate_probs[:, 1:2]).astype(bf16),
        ],
        axis=0,
    )
    send_grad = fold(
        *(
            matmul(jnp.concatenate(pair, axis=1), scaled).astype(bf16)
            for pair in zip(chosen(first), chosen(second), strict=True)
        )
    )
    local_x = routed(send_x)

    hidden_units = w_gate.shape[1]
    width = -(-hidden_units // LANES) * LANES
    pad = ((0, 0), (0, width - hidden_units))
    w_both = jnp.concatenate([jnp.pad(w_gate, pad), jnp.pad(w_up, pad)], axis=1)
    parts = matmul(local_x, w_both).astype(bf16)
    parts, send_grad = lax.optimization_barrier((parts, send_grad))
    sums = lax.psum_scatter(parts, "tensor", scatter_dimension=0, tiled=True)
    gate, up = (sums[:, k * width : (k + 1) * width].astype(jnp.float32) for k in range(2))

    local_grad = routed(send_grad)
    shards = lax.axis_size("tensor")
    pieces = matmul(local_grad, jnp.pad(w_down, pad[::-1]), 1, 1).astype(bf16)
    pieces = lax.all_to_all(
        pieces.reshape(shards, pieces.shape[0] // shards, width),
        "tensor",
        split_axis=0,
        concat_axis=0,
        tiled=True,
    )
    grad_hidden = jnp.sum(pieces.astype(jnp.float32), axis=0)
    hidden, grad_act_gate, grad_act_up = activations(gate, up, grad_hidden)

    def spread(part):
        return lax.all_gather(part, "tensor", axis=0, tiled=True)

    cut = hidden_units - LANES
    most = spread(hidden[:, :cut])
    acts = spread(
        jnp.concatenate([grad_act_gate, grad_act_up, hidden[:, cut:hidden_units]], axis=1)
    )
    most, acts = lax.optimization_barrier((most, acts))
    acts, least = acts[:, : 2 * width], acts[:, 2 * width :]
    grad_down = jnp.concatenate(
        [matmul(part, local_grad, 0, 0).astype(bf16) for part in (most, least)], axis=0
    )
    grad_gate = matmul(local_x, acts[:, :hidden_units], 0, 0).astype(bf16)
    grad_up = matmul(local_x, acts[:, width : width + hidden_units], 0, 0).astype(bf16)

    away = matmul(acts[half:], w_both, 1, 1).astype(bf16)
    away, acts = lax.optimization_barrier((away, acts))
    here = lax.optimization_barrier(matmul(acts[:half], w_both, 1, 1))
    away = lax.ppermute(away, "expert", other_core)
    chip_rows = (here + away.astype(jnp.float32)).astype(bf16)
    returned = jnp.concatenate(unfold(exchange(fold(chip_rows[:main], chip_rows[main:]))), axis=0)
    taking = jnp.concatenate(chosen(named), axis=0)
    grad_tokens = matmul(taking, returned, 0, 0).astype(bf16)
    return (grad_tokens, grad_gate, grad_up, grad_down)


def solution(mesh):
    placed = (
        P("expert", "tensor"),
        P("expert", "tensor"),
        P("expert", None),
        P("expert", None),
        P("tensor", "expert"),
        P("tensor", "expert"),
        P("expert", "tensor"),
    )
    return jax.shard_map(
        on_device,
        mesh=mesh,
        in_specs=placed,
        out_specs=(
            P("expert", "tensor"),
            P("tensor", "expert"),
            P("tensor", "expert"),
            P("expert", "tensor"),
        ),
        check_vma=False,
    )
```

```python
import jax
import jax.numpy as jnp
from jax import lax
from jax.sharding import PartitionSpec as P

MEMBERS = 4
CORES = 2
MAIN = 16
SUBLANES = 8
LANES = 128


def activations(gate, up, grad_hidden):
    sigma = jax.nn.sigmoid(gate)
    silu = gate * sigma
    hidden = (silu * up).astype(jnp.bfloat16)
    grad_act_gate = (grad_hidden * up * sigma * (1.0 + gate * (1.0 - sigma))).astype(jnp.bfloat16)
    grad_act_up = (grad_hidden * silu).astype(jnp.bfloat16)
    return (hidden, grad_act_gate, grad_act_up)


def matmul(a, b, a_dim=1, b_dim=0):
    return lax.dot_general(
        a, b, (((a_dim,), (b_dim,)), ((), ())), preferred_element_type=jnp.float32
    )


def on_device(tokens, out_grad, expert_ids, gate_probs, w_gate, w_up, w_down):
    bf16 = jnp.bfloat16
    count, columns = tokens.shape
    devices = lax.axis_size("expert")
    chips = devices // CORES
    groups = devices // MEMBERS
    same_core = [[core + CORES * chip for chip in range(chips)] for core in range(CORES)]
    other_core = [(device, device ^ 1) for device in range(devices)]

    ids = expert_ids.T
    experts = jnp.arange(groups, dtype=jnp.int32)[:, None]
    first, second = ids[0][None, :] == experts, ids[1][None, :] == experts
    named = first | second
    before = (
        jnp.arange(count, dtype=jnp.int32)[:, None] < jnp.arange(count, dtype=jnp.int32)[None, :]
    )
    rank = matmul(named.astype(bf16), before.astype(bf16)).astype(jnp.int32)
    place = jnp.where(named, rank, -1)

    main_slot = jnp.arange(MAIN, dtype=jnp.int32)[None, :, None]

    def chosen(mask):
        held = jnp.where(mask, place, -1)
        main = jnp.broadcast_to(
            (held[:, None, :] == main_slot)[:, None], (groups, CORES, MAIN, count)
        ).reshape(chips * MAIN, count)
        last = jnp.broadcast_to((held == MAIN)[:, None], (groups, CORES, count))
        return main.astype(bf16), last.reshape(chips, count).astype(bf16)

    blocks = columns // LANES
    tiles = MAIN // SUBLANES

    def fold(main, last):
        main = main.reshape(chips, tiles, SUBLANES, blocks, LANES).transpose(0, 1, 3, 2, 4)
        main = main.reshape(chips, MAIN * blocks, LANES)
        last = last.reshape(chips, blocks, LANES)
        spare = jnp.zeros((chips, -blocks % SUBLANES, LANES), last.dtype)
        return jnp.concatenate([main, last, spare], axis=1)

    def unfold(rows):
        main = rows[:, : MAIN * blocks].reshape(chips, tiles, blocks, SUBLANES, LANES)
        main = main.transpose(0, 1, 3, 2, 4).reshape(chips * MAIN, columns)
        return main, rows[:, MAIN * blocks : MAIN * blocks + blocks].reshape(chips, columns)

    def exchange(rows):
        return lax.all_to_all(
            rows, "expert", split_axis=0, concat_axis=0, tiled=True, axis_index_groups=same_core
        )

    def swapped(array):
        return lax.ppermute(array, "expert", other_core)

    def received(send):
        return jnp.concatenate(unfold(exchange(send)), axis=0)

    main = chips * MAIN
    half = main + chips
    send_x = fold(*(matmul(part, tokens).astype(bf16) for part in chosen(named)))
    send_x, out_grad, gate_probs = lax.optimization_barrier((send_x, out_grad, gate_probs))
    wide = out_grad.astype(jnp.float32)
    scaled = jnp.concatenate(
        [
            (wide * gate_probs[:, 0:1]).astype(bf16),
            (wide * gate_probs[:, 1:2]).astype(bf16),
        ],
        axis=0,
    )
    send_grad = fold(
        *(
            matmul(jnp.concatenate(pair, axis=1), scaled).astype(bf16)
            for pair in zip(chosen(first), chosen(second), strict=True)
        )
    )

    hidden_units = w_gate.shape[1]
    width = -(-hidden_units // LANES) * LANES
    pad = ((0, 0), (0, width - hidden_units))
    w_both = jnp.concatenate([jnp.pad(w_gate, pad), jnp.pad(w_up, pad)], axis=1)
    w_back = jnp.pad(w_down, pad[::-1])
    w_both_other, w_back_other = swapped(w_both), swapped(w_back)

    local_x = received(send_x)
    parts = jnp.concatenate(
        [matmul(local_x, w).astype(bf16) for w in (w_both, w_both_other)], axis=0
    )
    parts, send_grad = lax.optimization_barrier((parts, send_grad))
    sums = lax.psum_scatter(parts, "tensor", scatter_dimension=0, tiled=True)
    gate, up = (sums[:, k * width : (k + 1) * width].astype(jnp.float32) for k in range(2))

    local_grad = received(send_grad)
    shards = lax.axis_size("tensor")
    pieces = jnp.concatenate(
        [matmul(local_grad, w, 1, 1).astype(bf16) for w in (w_back, w_back_other)], axis=0
    )
    pieces = lax.all_to_all(
        pieces.reshape(shards, pieces.shape[0] // shards, width),
        "tensor",
        split_axis=0,
        concat_axis=0,
        tiled=True,
    )
    grad_hidden = jnp.sum(pieces.astype(jnp.float32), axis=0)
    hidden, grad_act_gate, grad_act_up = activations(gate, up, grad_hidden)

    def spread(part):
        return lax.all_gather(part, "tensor", axis=0, tiled=True)

    cut = hidden_units - LANES
    most = spread(hidden[:, :cut])
    acts = spread(
        jnp.concatenate([grad_act_gate, grad_act_up, hidden[:, cut:hidden_units]], axis=1)
    )

    most, local_x, local_grad = lax.optimization_barrier((most, local_x, local_grad))

    def both_cores(own, other):
        return jnp.concatenate([own, other], axis=0)

    all_x = both_cores(local_x, swapped(local_x))
    all_grad = both_cores(local_grad, swapped(local_grad))
    all_most = both_cores(most[:half], swapped(most[half:]))
    down = matmul(all_most, all_grad, 0, 0).astype(bf16)
    down, all_x, all_grad, acts = lax.optimization_barrier((down, all_x, all_grad, acts))

    rows = matmul(acts[:half, : 2 * width], w_both, 1, 1)
    rows = rows + matmul(acts[half:, : 2 * width], w_both_other, 1, 1)
    rows = rows.astype(bf16)
    send_back = fold(rows[:main], rows[main:])
    send_back, acts = lax.optimization_barrier((send_back, acts))
    returned = exchange(send_back)
    all_acts = both_cores(acts[:half], swapped(acts)[half:])
    grad_gate = matmul(all_x, all_acts[:, :hidden_units], 0, 0).astype(bf16)
    grad_up = matmul(all_x, all_acts[:, width : width + hidden_units], 0, 0).astype(bf16)
    least = matmul(all_acts[:, 2 * width :], all_grad, 0, 0).astype(bf16)
    grad_down = jnp.concatenate([down, least], axis=0)
    returned, grad_gate, grad_up, grad_down = lax.optimization_barrier(
        (returned, grad_gate, grad_up, grad_down)
    )
    returned = jnp.concatenate(unfold(returned), axis=0)
    taking = jnp.concatenate(chosen(named), axis=0)
    grad_tokens = matmul(taking, returned, 0, 0).astype(bf16)
    return (grad_tokens, grad_gate, grad_up, grad_down)


def solution(mesh):
    placed = (
        P("expert", "tensor"),
        P("expert", "tensor"),
        P("expert", None),
        P("expert", None),
        P("tensor", "expert"),
        P("tensor", "expert"),
        P("expert", "tensor"),
    )
    return jax.shard_map(
        on_device,
        mesh=mesh,
        in_specs=placed,
        out_specs=(
            P("expert", "tensor"),
            P("tensor", "expert"),
            P("tensor", "expert"),
            P("expert", "tensor"),
        ),
        check_vma=False,
    )
```

```python
import jax
import jax.numpy as jnp
from jax import lax
from jax.sharding import PartitionSpec as P

MEMBERS = 4
CORES = 2
MAIN = 16
SUBLANES = 8
LANES = 128


def activations(gate, up, grad_hidden):
    sigma = jax.nn.sigmoid(gate)
    silu = gate * sigma
    hidden = (silu * up).astype(jnp.bfloat16)
    grad_act_gate = (grad_hidden * up * sigma * (1.0 + gate * (1.0 - sigma))).astype(jnp.bfloat16)
    grad_act_up = (grad_hidden * silu).astype(jnp.bfloat16)
    return (hidden, grad_act_gate, grad_act_up)


def matmul(a, b, a_dim=1, b_dim=0):
    return lax.dot_general(
        a, b, (((a_dim,), (b_dim,)), ((), ())), preferred_element_type=jnp.float32
    )


def on_device(tokens, out_grad, expert_ids, gate_probs, w_gate, w_up, w_down):
    bf16 = jnp.bfloat16
    count, columns = tokens.shape
    devices = lax.axis_size("expert")
    chips = devices // CORES
    groups = devices // MEMBERS
    same_core = [[core + CORES * chip for chip in range(chips)] for core in range(CORES)]
    other_core = [(device, device ^ 1) for device in range(devices)]

    ids = expert_ids.T
    experts = jnp.arange(groups, dtype=jnp.int32)[:, None]
    first, second = ids[0][None, :] == experts, ids[1][None, :] == experts
    named = first | second
    before = (
        jnp.arange(count, dtype=jnp.int32)[:, None] < jnp.arange(count, dtype=jnp.int32)[None, :]
    )
    rank = matmul(named.astype(bf16), before.astype(bf16)).astype(jnp.int32)
    place = jnp.where(named, rank, -1)

    main_slot = jnp.arange(MAIN, dtype=jnp.int32)[None, :, None]

    def chosen(mask):
        held = jnp.where(mask, place, -1)
        main = jnp.broadcast_to(
            (held[:, None, :] == main_slot)[:, None], (groups, CORES, MAIN, count)
        ).reshape(chips * MAIN, count)
        last = jnp.broadcast_to((held == MAIN)[:, None], (groups, CORES, count))
        return main.astype(bf16), last.reshape(chips, count).astype(bf16)

    blocks = columns // LANES
    tiles = MAIN // SUBLANES

    def fold(main, last):
        main = main.reshape(chips, tiles, SUBLANES, blocks, LANES).transpose(0, 1, 3, 2, 4)
        main = main.reshape(chips, MAIN * blocks, LANES)
        last = last.reshape(chips, blocks, LANES)
        spare = jnp.zeros((chips, -blocks % SUBLANES, LANES), last.dtype)
        return jnp.concatenate([main, last, spare], axis=1)

    def unfold(rows):
        main = rows[:, : MAIN * blocks].reshape(chips, tiles, blocks, SUBLANES, LANES)
        main = main.transpose(0, 1, 3, 2, 4).reshape(chips * MAIN, columns)
        return main, rows[:, MAIN * blocks : MAIN * blocks + blocks].reshape(chips, columns)

    def exchange(rows):
        return lax.all_to_all(
            rows, "expert", split_axis=0, concat_axis=0, tiled=True, axis_index_groups=same_core
        )

    def swapped(array):
        return lax.ppermute(array, "expert", other_core)

    def received(send):
        return jnp.concatenate(unfold(exchange(send)), axis=0)

    main = chips * MAIN
    half = main + chips
    send_x = fold(*(matmul(part, tokens).astype(bf16) for part in chosen(named)))
    send_x, out_grad, gate_probs = lax.optimization_barrier((send_x, out_grad, gate_probs))
    wide = out_grad.astype(jnp.float32)
    scaled = jnp.concatenate(
        [
            (wide * gate_probs[:, 0:1]).astype(bf16),
            (wide * gate_probs[:, 1:2]).astype(bf16),
        ],
        axis=0,
    )
    send_grad = fold(
        *(
            matmul(jnp.concatenate(pair, axis=1), scaled).astype(bf16)
            for pair in zip(chosen(first), chosen(second), strict=True)
        )
    )

    hidden_units = w_gate.shape[1]
    width = -(-hidden_units // LANES) * LANES
    pad = ((0, 0), (0, width - hidden_units))
    w_both = jnp.concatenate([jnp.pad(w_gate, pad), jnp.pad(w_up, pad)], axis=1)
    w_back = jnp.pad(w_down, pad[::-1])
    w_both_other, w_back_other = swapped(w_both), swapped(w_back)

    local_x = received(send_x)
    parts = jnp.concatenate(
        [matmul(local_x, w).astype(bf16) for w in (w_both, w_both_other)], axis=0
    )
    parts, send_grad = lax.optimization_barrier((parts, send_grad))
    sums = lax.psum_scatter(parts, "tensor", scatter_dimension=0, tiled=True)
    gate, up = (sums[:, k * width : (k + 1) * width].astype(jnp.float32) for k in range(2))

    local_grad = received(send_grad)
    shards = lax.axis_size("tensor")
    pieces = lax.dot_general(
        jnp.broadcast_to(local_grad, (CORES, *local_grad.shape)),
        jnp.stack([w_back, w_back_other]),
        (((2,), (2,)), ((0,), (0,))),
        preferred_element_type=jnp.float32,
    )
    pieces = pieces.astype(bf16).reshape(CORES * half, width)
    pieces = lax.all_to_all(
        pieces.reshape(shards, pieces.shape[0] // shards, width),
        "tensor",
        split_axis=0,
        concat_axis=0,
        tiled=True,
    )
    grad_hidden = jnp.sum(pieces.astype(jnp.float32), axis=0)
    hidden, grad_act_gate, grad_act_up = activations(gate, up, grad_hidden)

    def spread(part):
        return lax.all_gather(part, "tensor", axis=0, tiled=True)

    cut = hidden_units - LANES
    most = spread(hidden[:, :cut])
    acts = spread(
        jnp.concatenate([grad_act_gate, grad_act_up, hidden[:, cut:hidden_units]], axis=1)
    )

    most, local_x, local_grad = lax.optimization_barrier((most, local_x, local_grad))

    def both_cores(own, other):
        return jnp.concatenate([own, other], axis=0)

    all_x = both_cores(local_x, swapped(local_x))
    all_grad = both_cores(local_grad, swapped(local_grad))
    all_most = both_cores(most[:half], swapped(most[half:]))
    down = matmul(all_most, all_grad, 0, 0).astype(bf16)
    down, all_x, all_grad, acts = lax.optimization_barrier((down, all_x, all_grad, acts))

    rows = matmul(acts[:half, : 2 * width], w_both, 1, 1)
    rows = rows + matmul(acts[half:, : 2 * width], w_both_other, 1, 1)
    rows = rows.astype(bf16)
    send_back = fold(rows[:main], rows[main:])
    send_back, acts = lax.optimization_barrier((send_back, acts))
    returned = exchange(send_back)
    all_acts = both_cores(acts[:half], swapped(acts)[half:])
    grad_gate = matmul(all_x, all_acts[:, :hidden_units], 0, 0).astype(bf16)
    grad_up = matmul(all_x, all_acts[:, width : width + hidden_units], 0, 0).astype(bf16)
    least = matmul(all_acts[:, 2 * width :], all_grad, 0, 0).astype(bf16)
    grad_down = jnp.concatenate([down, least], axis=0)
    returned, grad_gate, grad_up, grad_down = lax.optimization_barrier(
        (returned, grad_gate, grad_up, grad_down)
    )
    returned = jnp.concatenate(unfold(returned), axis=0)
    taking = jnp.concatenate(chosen(named), axis=0)
    grad_tokens = matmul(taking, returned, 0, 0).astype(bf16)
    return (grad_tokens, grad_gate, grad_up, grad_down)


def solution(mesh):
    placed = (
        P("expert", "tensor"),
        P("expert", "tensor"),
        P("expert", None),
        P("expert", None),
        P("tensor", "expert"),
        P("tensor", "expert"),
        P("expert", "tensor"),
    )
    return jax.shard_map(
        on_device,
        mesh=mesh,
        in_specs=placed,
        out_specs=(
            P("expert", "tensor"),
            P("tensor", "expert"),
            P("tensor", "expert"),
            P("expert", "tensor"),
        ),
        check_vma=False,
    )
```
